128 devices in a mesh: row: 16 (over y_lo, z, core), col: 8 (over x, y_hi).
Axes of the slice: x: 4, y: 4 (y_hi: 2, y_lo: 2; y = y_hi * 2 + y_lo), z: 4, core: 2. Of those that a mesh axis runs over, the one named last changes fastest.
Arguments:
- pair: bfloat16 [768, 768, 128], P('row', 'col'), may hold values from -4 to 4
- token_mask: int32 [768], replicated, may hold values from 0 to 1, as said below
- chain_ids: int32 [768], replicated, may hold values from 0 to 3, as said below
- w_query: bfloat16 [128, 128], replicated, may hold values from -0.5 to 0.5
- w_key: bfloat16 [128, 128], replicated, may hold values from -0.5 to 0.5
- w_value: bfloat16 [128, 128], replicated, may hold values from -0.5 to 0.5
- w_gate: bfloat16 [128, 128], replicated, may hold values from -0.5 to 0.5
- w_bias: bfloat16 [128, 4], replicated, may hold values from -2.5 to 2.5
- w_out: bfloat16 [128, 128], replicated, may hold values from -6 to 6
Outputs:
- update: bfloat16 [768, 768, 128], P('row', 'col')
The draws below stay inside these ranges and needn't reach their ends.
Inputs may be any that keep to these rules, and one draw needn't show every extreme that they name: `token_mask`: 0 or 1; the first token of every chain is 1. `chain_ids`: never falling along the tokens, every chain nonempty; chain 0 holds at least the first 385 tokens.
All inputs are finite; a program needn't handle non-finite values.
Results may differ from the reference program's by a relative error of at most 0.0095.
Values may be sent and summed in bfloat16 or wider, within the bound.
A program may use at most 192 MiB of HBM per device.

```python
import math
import jax
import jax.numpy as jnp
from jax import lax

C = 128
HEADS = 4
HEAD_DIM = 32
TOKENS = 768


def chain_bounds(key):
    first_key, second_key, third_key = jax.random.split(key, 3)
    first = TOKENS // 2 + 1 + jax.random.randint(first_key, (), 0, TOKENS // 4)
    second = first + jax.random.randint(second_key, (), 1, TOKENS - first - 1)
    third = second + jax.random.randint(third_key, (), 1, TOKENS - second)
    return (first, second, third)


def draw_chain_ids(key, part):
    first, second, third = chain_bounds(key)
    position = jnp.arange(TOKENS, dtype=jnp.int32)
    chains = (position >= first).astype(jnp.int32) + (position >= second).astype(jnp.int32)
    return chains + (position >= third).astype(jnp.int32)


def draw_token_mask(key, part):
    first, second, third = chain_bounds(key)
    key = jax.random.fold_in(key, 5)
    position = jnp.arange(TOKENS, dtype=jnp.int32)
    keeping = jax.random.randint(key, (TOKENS,), 0, 8) < 7
    starts = (position == 0) | (position == first) | (position == second) | (position == third)
    return (keeping | starts).astype(jnp.int32)


def draw_pair(key, part):
    key = jax.random.fold_in(key, 7)
    base_key = jax.random.fold_in(key, 0)
    return jnp.clip(jax.random.normal(base_key, (TOKENS, TOKENS, C), jnp.float32), -4.0, 4.0).astype(jnp.bfloat16)


def draw_w_bias(key, part):
    key = jax.random.fold_in(key, 11)
    noise = jnp.clip(jax.random.normal(key, (C, HEADS), jnp.float32), -3.0, 3.0)
    return (noise / jnp.sqrt(jnp.float32(C))).astype(jnp.bfloat16)


def gaussian(stream_key, shape, scale, reach, held_as=jnp.bfloat16):
    return jnp.clip(scale * jax.random.normal(stream_key, shape, jnp.float32), -reach, reach).astype(held_as)


def setup_inputs(seed: int = 0) -> dict:
    splits = jax.random.split(jax.random.key(seed), 10)
    pair = draw_pair(jax.random.fold_in(splits[9], 71), 0)
    token_mask = draw_token_mask(jax.random.fold_in(splits[9], 71), 0)
    chain_ids = draw_chain_ids(jax.random.fold_in(splits[9], 71), 0)
    w_query = gaussian(splits[3], (C, HEADS * HEAD_DIM), C ** -0.5, 0.5)
    w_key = gaussian(splits[4], (C, HEADS * HEAD_DIM), C ** -0.5, 0.5)
    w_value = gaussian(splits[5], (C, HEADS * HEAD_DIM), C ** -0.5, 0.5)
    w_gate = gaussian(splits[6], (C, HEADS * HEAD_DIM), C ** -0.5, 0.5)
    w_bias = draw_w_bias(jax.random.fold_in(splits[9], 71), 0)
    w_out = gaussian(splits[8], (HEADS * HEAD_DIM, C), 1.0, 6.0)
    return {"pair": pair, "token_mask": token_mask, "chain_ids": chain_ids, "w_query": w_query, "w_key": w_key, "w_value": w_value, "w_gate": w_gate, "w_bias": w_bias, "w_out": w_out}


def normalize(pair):
    values = pair.astype(jnp.float32)
    center = lax.optimization_barrier(jnp.mean(values, axis=-1, keepdims=True))
    spread = lax.optimization_barrier(jnp.mean((values - center) ** 2, axis=-1, keepdims=True))
    return ((values - center) * lax.rsqrt(spread + 1e-05)).astype(jnp.bfloat16)

def reference(pair, token_mask, chain_ids, w_query, w_key, w_value, w_gate, w_bias, w_out):
    normed = normalize(pair)
    flat = normed.reshape(TOKENS * TOKENS, C)
    inner = HEADS * HEAD_DIM
    factor = 1.0 / math.sqrt(HEAD_DIM)
    query = (jnp.dot(flat, w_query, preferred_element_type=jnp.float32) * factor).astype(jnp.bfloat16)
    key = jnp.dot(flat, w_key, preferred_element_type=jnp.float32).astype(jnp.bfloat16)
    value = jnp.dot(flat, w_value, preferred_element_type=jnp.float32).astype(jnp.bfloat16)
    gate = jax.nn.sigmoid(jnp.dot(flat, w_gate, preferred_element_type=jnp.float32)).reshape(TOKENS, TOKENS, inner)
    bias = jnp.dot(flat, w_bias, preferred_element_type=jnp.float32).astype(jnp.bfloat16).reshape(TOKENS, TOKENS, HEADS)
    bias_t = jnp.transpose(bias, (2, 1, 0)).astype(jnp.float32)
    query = query.reshape(TOKENS, TOKENS, HEADS, HEAD_DIM)
    key = key.reshape(TOKENS, TOKENS, HEADS, HEAD_DIM)
    value = value.reshape(TOKENS, TOKENS, HEADS, HEAD_DIM)
    allowed = (token_mask[:, None] == 1) & (chain_ids[:, None] == chain_ids[None, :])
    width = math.gcd(TOKENS, 16)

    def column_block(block_index):
        first = (block_index * width).astype(jnp.int32)
        q_block = lax.dynamic_slice_in_dim(query, first, width, 1).astype(jnp.float32)
        k_block = lax.dynamic_slice_in_dim(key, first, width, 1).astype(jnp.float32)
        v_block = lax.dynamic_slice_in_dim(value, first, width, 1).astype(jnp.float32)
        keep = lax.dynamic_slice_in_dim(allowed, first, width, 1)
        scores = jnp.einsum('ibhd,kbhd->bhik', q_block, k_block) + bias_t[None]
        scores = jnp.where(jnp.transpose(keep)[:, None, None, :], scores, jnp.float32(-1e+30))
        peak = lax.optimization_barrier(jnp.max(scores, axis=-1, keepdims=True))
        weights = jnp.exp(scores - peak)
        total = lax.optimization_barrier(jnp.sum(weights, axis=-1))
        mixed = jnp.einsum('bhik,kbhd->bhid', weights.astype(jnp.bfloat16).astype(jnp.float32), v_block)
        mixed = mixed / total[..., None]
        return jnp.transpose(mixed, (2, 0, 1, 3))
    blocks = lax.map(column_block, jnp.arange(TOKENS // width, dtype=jnp.int32))
    attended = jnp.transpose(blocks, (1, 0, 2, 3, 4)).reshape(TOKENS, TOKENS, inner)
    gated = (gate * attended).astype(jnp.bfloat16)
    update = jnp.dot(gated.reshape(TOKENS * TOKENS, inner), w_out, preferred_element_type=jnp.float32)
    return update.astype(jnp.bfloat16).reshape(TOKENS, TOKENS, C)
```

```python
import functools
import math

import jax
import jax.numpy as jnp
from jax import lax
from jax.experimental import pallas as pl
from jax.experimental.pallas import tpu as pltpu
from jax.sharding import PartitionSpec as P

LOG2E = math.log2(math.e)
NT = (((1,), (1,)), ((), ()))
NEG = -1e30


def normalize(pair):
    values = pair.astype(jnp.float32)
    center = jnp.mean(values, axis=-1, keepdims=True)
    spread = jnp.mean((values - center) ** 2, axis=-1, keepdims=True)
    return ((values - center) * lax.rsqrt(spread + 1e-05)).astype(jnp.bfloat16)


def attend(heads, x_ref, bias_ref, mask_ref, wqg_ref, wkt_ref, wv_ref, wo_ref, out_ref, kt, va, q_s, g_s, acc):
    ncol, count, width = x_ref.shape
    head_dim = width // heads
    lane = lax.broadcasted_iota(jnp.int32, (count, width), 1) // head_dim
    kt[...] = jnp.zeros_like(kt)
    va[:, width:] = jnp.ones((count, width), jnp.bfloat16)
    q_s[:, width:] = (lax.broadcasted_iota(jnp.int32, (count, width), 1) == 0).astype(jnp.bfloat16)

    def column(j, _):
        x = x_ref[j]
        qg = jnp.dot(x, wqg_ref[...], preferred_element_type=jnp.float32)
        q = qg[:, :width] * (LOG2E / math.sqrt(head_dim))
        g_s[...] = jax.nn.sigmoid(qg[:, width:])
        kt[:width, :] = lax.dot_general(wkt_ref[...], x, NT, preferred_element_type=jnp.float32).astype(jnp.bfloat16)
        first = lax.broadcasted_iota(jnp.int32, (16, count), 0) == 0
        kt[width : width + 16, :] = jnp.where(first, mask_ref[pl.ds(j, 1), :], 0.0).astype(jnp.bfloat16)
        va[:, :width] = jnp.dot(x, wv_ref[...], preferred_element_type=jnp.float32).astype(jnp.bfloat16)
        for h in range(heads):
            q_s[:, :width] = jnp.where(lane == h, q, 0.0).astype(jnp.bfloat16)
            s = jnp.dot(q_s[...], kt[...], preferred_element_type=jnp.float32)
            s = s + bias_ref[h].astype(jnp.float32) * LOG2E
            peak = jnp.max(s, axis=1, keepdims=True)
            p = jnp.exp2(s - peak).astype(jnp.bfloat16)
            o = jnp.dot(p, va[...], preferred_element_type=jnp.float32)
            acc[...] = o if h == 0 else jnp.where(jnp.concatenate([lane, lane], 1) == h, o, acc[...])
        o = acc[...]
        gated = (o[:, :width] / o[:, width:] * g_s[...]).astype(jnp.bfloat16)
        out_ref[j] = jnp.dot(gated, wo_ref[...], preferred_element_type=jnp.float32).astype(jnp.bfloat16)
        return 0

    lax.fori_loop(0, ncol, column, 0)


def attention(heads, x, bias, mask, wqg, wkt, wv, wo):
    ncol, count, width = x.shape
    return pl.pallas_call(
        functools.partial(attend, heads),
        out_shape=jax.ShapeDtypeStruct(x.shape, jnp.bfloat16),
        in_specs=[pl.BlockSpec(memory_space=pltpu.VMEM)] * 7,
        out_specs=pl.BlockSpec(memory_space=pltpu.VMEM),
        scratch_shapes=[
            pltpu.VMEM((2 * width, count), jnp.bfloat16),
            pltpu.VMEM((count, 2 * width), jnp.bfloat16),
            pltpu.VMEM((count, 2 * width), jnp.bfloat16),
            pltpu.VMEM((count, width), jnp.float32),
            pltpu.VMEM((count, 2 * width), jnp.float32),
        ],
        compiler_params=pltpu.CompilerParams(vmem_limit_bytes=52 * 2**20),
    )(x, bias, mask, wqg, wkt, wv, wo)


def body(pair, token_mask, chain_ids, w_query, w_key, w_value, w_gate, w_bias, w_out):
    rows, cols, width = pair.shape
    heads = w_bias.shape[1]
    count = token_mask.shape[0]
    members = count // rows
    mine = cols // members
    normed = jnp.swapaxes(normalize(pair), 0, 1)
    x = lax.all_to_all(normed, "row", 0, 1, tiled=True)
    first = lax.axis_index("col") * cols + lax.axis_index("row") * mine
    bias = lax.dot_general(w_bias, x, (((0,), (2,)), ((), ())), preferred_element_type=jnp.float32).astype(jnp.bfloat16)
    bias = lax.all_gather(bias, ("col", "row"), axis=1, tiled=True)
    my_chain = lax.dynamic_slice_in_dim(chain_ids, first, mine)
    keep = (token_mask == 1)[None, :] & (chain_ids[None, :] == my_chain[:, None])
    mask = jnp.where(keep, 0.0, NEG).astype(jnp.float32)
    update = attention(heads, x, bias, mask, jnp.concatenate([w_query, w_gate], 1), w_key.T, w_value, w_out)
    update = lax.all_to_all(update, "row", 1, 0, tiled=True)
    return jnp.swapaxes(update, 0, 1)


def solution(mesh):
    placed = (P("row", "col", None), P(), P(), P(), P(), P(), P(), P(), P())
    return jax.shard_map(
        body, mesh=mesh, in_specs=placed, out_specs=P("row", "col", None), check_vma=False
    )
```

```python
import functools
import math

import jax
import jax.numpy as jnp
from jax import lax
from jax.experimental import pallas as pl
from jax.experimental.pallas import tpu as pltpu
from jax.sharding import PartitionSpec as P

LOG2E = math.log2(math.e)
NT = (((1,), (1,)), ((), ()))
NEG = -1e30
MESH = pl.DeviceIdType.MESH
Z, X, Y = 4, 4, 4
GROUP = 3


def kernel(
    heads,
    pair_ref, mask_ref, wqg_ref, wkt_ref, wv_ref, wbt_ref, wo_ref, out_ref,
    normed, bias_f32, sent, x_ref, tiles, bias, q_s, g_s, kt, va, acc, back,
    in_send, in_recv, z_send, z_recv, y_send, y_recv, x1_send, x1_recv, x2_send, x2_recv,
    sib_send, sib_recv, out_send, out_recv,
):
    rows, cols, width = pair_ref.shape
    ncol, count, _ = x_ref.shape
    head_dim = width // heads
    members = count // rows
    half = count // 2
    row, col = lax.axis_index("row"), lax.axis_index("col")
    core, z, y_lo = lax.rem(row, 2), lax.rem(row // 2, Z), row // (2 * Z)
    x, y_hi = col // 2, lax.rem(col, 2)
    y = y_hi * 2 + y_lo
    place = row // 2
    slot = core * (members // 2) + place
    sibling = (row + 1 - 2 * core, col)
    right, left = (row, lax.rem(x + 1, X) * 2 + y_hi), (row, lax.rem(x + X - 1, X) * 2 + y_hi)
    x_left, x_right, x_far = lax.rem(x + X - 1, X), lax.rem(x + 1, X), lax.rem(x + 2, X)

    def y_peer(step):
        there = lax.rem(y + step, Y)
        return ((lax.rem(there, 2) * Z + z) * 2 + core, x * 2 + there // 2)

    def send(src, dst, send_sem, recv_sem, device):
        pltpu.make_async_remote_copy(
            src_ref=src, dst_ref=dst, send_sem=send_sem, recv_sem=recv_sem, device_id=device, device_id_type=MESH
        ).start()

    def await_bytes(ref, sem):
        pltpu.make_async_copy(ref, ref, sem).wait()

    barrier = pltpu.get_barrier_semaphore()

    def greet(step, _):
        pl.semaphore_signal(barrier, inc=1, device_id=(lax.rem(row + step, members), col), device_id_type=MESH)
        return 0

    lax.fori_loop(1, members, greet, 0)
    for device in (right, left, y_peer(2), y_peer(3 - 2 * y_lo)):
        pl.semaphore_signal(barrier, inc=1, device_id=device, device_id_type=MESH)

    bias_f32[...] = jnp.zeros_like(bias_f32)
    many = 4

    def norm(t, _):
        values = pair_ref[pl.ds(t * many, many)].reshape(many * cols, width).astype(jnp.float32)
        center = jnp.mean(values, axis=-1, keepdims=True)
        spread = jnp.mean((values - center) ** 2, axis=-1, keepdims=True)
        block = ((values - center) * lax.rsqrt(spread + 1e-05)).astype(jnp.bfloat16)
        normed[pl.ds(pl.multiple_of(t * many * cols, many * cols), many * cols), :] = block.astype(jnp.float32)
        for u in range(many):
            part = block[u * cols : (u + 1) * cols]
            line = lax.dot_general(wbt_ref[...], part, NT, preferred_element_type=jnp.float32)
            bias_f32[pl.ds(pl.multiple_of((t * many + u) * 8, 8), 8), :cols] = line[:8]
        return 0

    lax.fori_loop(0, rows // many, norm, 0)
    mine = pl.ds(pl.multiple_of(place * rows, rows), rows)
    for h in range(heads):
        tiles[h, y_hi, mine, :] = bias_f32[pl.ds(h, rows, stride=8), :].astype(jnp.bfloat16)

    pl.semaphore_wait(barrier, members + 3)
    for step in range(1, Z):
        there = (row - 2 * z + 2 * lax.rem(z + step, Z), col)
        send(tiles.at[:, y_hi, mine], tiles.at[:, y_hi, mine], z_send, z_recv, there)

    def turn(t, _):
        for u in range(many):
            j = t * many + u
            sent[j] = normed[pl.ds(j, rows, stride=cols), :].astype(jnp.bfloat16)
        return 0

    lax.fori_loop(0, cols // many, turn, 0)
    here = pl.ds(pl.multiple_of(slot * rows, rows), rows)
    for g in range(ncol // GROUP):
        def scatter(step, _, g=g):
            peer = lax.rem(row + step, members)
            send(
                sent.at[pl.ds(peer * ncol + g * GROUP, GROUP)],
                x_ref.at[pl.ds(g * GROUP, GROUP), here],
                in_send, in_recv.at[g], (peer, col),
            )
            return 0

        lax.fori_loop(1, members, scatter, 0)
    for j in range(ncol):
        x_ref[j, here, :] = sent[row * ncol + j]

    await_bytes(tiles.at[:, 0, pl.ds(0, (Z - 1) * rows)], z_recv)
    quarter = pl.ds(pl.multiple_of(y_lo * Z * rows, Z * rows), Z * rows)
    for h in range(heads):
        for step in range(1, Y):
            block = tiles.at[h, y_hi, quarter]
            send(block, block, y_send, y_recv.at[h, step - 1], y_peer(step))

    wide = cols // 2
    eye = (
        lax.broadcasted_iota(jnp.int32, (cols, 128), 0) == lax.broadcasted_iota(jnp.int32, (cols, 128), 1)
    ).astype(jnp.bfloat16)

    def owned(h, owner, part=slice(None)):
        return bias.at[h, core, part, pl.ds(pl.multiple_of(owner * cols, cols), cols)]

    for h in range(heads):
        for step in range(1, Y):
            await_bytes(tiles.at[h, 0, pl.ds(0, Z * rows)], y_recv.at[h, step - 1])
        for side in range(2):
            turned = lax.dot_general(eye, tiles[h, side], NT, preferred_element_type=jnp.float32).astype(jnp.bfloat16)
            for part in range(2):
                at = pl.ds(pl.multiple_of(x * cols + side * wide, wide), wide)
                bias[h, core, part, at, :] = turned[part * wide : (part + 1) * wide]
        block = owned(h, x)
        send(block, block, x1_send, x1_recv.at[h, 0], right)
        send(block, block, x1_send, x1_recv.at[h, 1], left)
        send(block, block, sib_send, sib_recv.at[h, 0], sibling)

    def forward(h):
        await_bytes(owned(h, x_left), x1_recv.at[h, 0])
        block = owned(h, x_left, 0)
        send(block, block, x2_send, x2_recv.at[h, 0], right)
        block = owned(h, x_left)
        send(block, block, sib_send, sib_recv.at[h, 1], sibling)
        await_bytes(owned(h, x_right), x1_recv.at[h, 1])
        block = owned(h, x_right, 1)
        send(block, block, x2_send, x2_recv.at[h, 1], left)
        block = owned(h, x_right)
        send(block, block, sib_send, sib_recv.at[h, 2], sibling)

    def pass_on(h):
        for part in range(2):
            block = owned(h, x_far, part)
            await_bytes(block, x2_recv.at[h, part])
            send(block, block, sib_send, sib_recv.at[h, 3 + part], sibling)

    def complete(h):
        for n in range(3):
            await_bytes(owned(h, x), sib_recv.at[h, n])
        for n in range(2):
            await_bytes(owned(h, x, 0), sib_recv.at[h, 3 + n])

    lane = lax.broadcasted_iota(jnp.int32, (count, width), 1) // head_dim
    one = (lax.broadcasted_iota(jnp.int32, (count, width), 1) == 0).astype(jnp.bfloat16)

    def project(j, _):
        block = x_ref[j]
        qg = jnp.dot(block, wqg_ref[...], preferred_element_type=jnp.float32)
        q_s[j] = (qg[:, :width] * (LOG2E / math.sqrt(head_dim))).astype(jnp.bfloat16)
        g_s[j] = jax.nn.sigmoid(qg[:, width:])
        kt[j, :width, :] = lax.dot_general(wkt_ref[...], block, NT, preferred_element_type=jnp.float32).astype(
            jnp.bfloat16
        )
        first = lax.broadcasted_iota(jnp.int32, (16, count), 0) == 0
        kt[j, width : width + 16, :] = jnp.where(first, mask_ref[pl.ds(j, 1), :], 0.0).astype(jnp.bfloat16)
        kt[j, width + 16 :, :] = jnp.zeros((width - 16, count), jnp.bfloat16)
        va[j, :, :width] = jnp.dot(block, wv_ref[...], preferred_element_type=jnp.float32).astype(jnp.bfloat16)
        va[j, :, width:] = jnp.ones((count, width), jnp.bfloat16)
        return 0

    for g in range(ncol // GROUP):
        await_bytes(x_ref.at[pl.ds(0, GROUP), pl.ds(0, count - rows)], in_recv.at[g])
        lax.fori_loop(g * GROUP, (g + 1) * GROUP, project, 0)
        if g == 0:
            forward(0)

    def attend(h, j):
        q = jnp.where(lane == h, q_s[j], jnp.zeros((count, width), jnp.bfloat16))
        s = jnp.dot(jnp.concatenate([q, one], 1), kt[j], preferred_element_type=jnp.float32)
        b = jnp.concatenate([bias[h, n].reshape(count, half) for n in range(2)], 1)
        s = s + b.astype(jnp.float32) * LOG2E
        peak = jnp.max(s, axis=1, keepdims=True)
        p = jnp.exp2(s - peak).astype(jnp.bfloat16)
        o = jnp.dot(p, va[j], preferred_element_type=jnp.float32)
        acc[j] = o if h == 0 else jnp.where(jnp.concatenate([lane, lane], 1) == h, o, acc[j])

    def only(h):
        def step(j, _):
            attend(h, j)
            return 0
        return step

    def last(j, _):
        attend(heads - 2, j)
        attend(heads - 1, j)
        o = acc[j]
        gated = (o[:, :width] / o[:, width:] * g_s[j]).astype(jnp.bfloat16)
        back[j] = jnp.dot(gated, wo_ref[...], preferred_element_type=jnp.float32).astype(jnp.bfloat16)

        def give(step, _):
            peer = lax.rem(row + step, members)
            at = (lax.rem(peer, 2) * (members // 2) + peer // 2) * rows
            send(
                back.at[j, pl.ds(pl.multiple_of(at, rows), rows)], out_ref.at[row * ncol + j],
                out_send, out_recv, (peer, col),
            )
            return 0

        lax.fori_loop(1, members, give, 0)
        out_ref[row * ncol + j] = back[j, here, :]
        return 0

    pass_on(0)
    forward(1)
    complete(0)
    lax.fori_loop(0, ncol // 2, only(0), 0)
    pass_on(1)
    forward(2)
    lax.fori_loop(ncol // 2, ncol, only(0), 0)
    complete(1)
    lax.fori_loop(0, ncol // 2, only(1), 0)
    pass_on(2)
    forward(3)
    lax.fori_loop(ncol // 2, ncol, only(1), 0)
    pass_on(3)
    complete(2)
    complete(3)
    lax.fori_loop(0, ncol, last, 0)

    await_bytes(out_ref.at[pl.ds(0, (members - 1) * ncol)], out_recv)
    await_bytes(out_ref.at[pl.ds(0, (members - 1) * ncol)], out_send)
    await_bytes(sent.at[pl.ds(0, (members - 1) * ncol)], in_send)
    await_bytes(tiles.at[:, 0, pl.ds(0, (Z - 1) * rows)], z_send)
    await_bytes(tiles.at[pl.ds(0, Y - 1)], y_send)
    await_bytes(bias.at[0], x1_send)
    await_bytes(bias.at[0, 0], x2_send)
    await_bytes(bias.at[:, 0], sib_send)


def exchange(heads, ncol, count, pair, mask, wqg, wkt, wv, wbt, wo):
    rows, cols, width = pair.shape
    half = count // 2
    bf16, f32 = jnp.bfloat16, jnp.float32
    dma = pltpu.SemaphoreType.DMA
    return pl.pallas_call(
        functools.partial(kernel, heads),
        out_shape=jax.ShapeDtypeStruct((cols, rows, width), bf16),
        in_specs=[pl.BlockSpec(memory_space=pltpu.VMEM)] * 7,
        out_specs=pl.BlockSpec(memory_space=pltpu.VMEM),
        scratch_shapes=[
            pltpu.VMEM((rows * cols, width), f32),
            pltpu.VMEM((rows * 8, 128), f32),
            pltpu.VMEM((cols, rows, width), bf16),
            pltpu.VMEM((ncol, count, width), bf16),
            pltpu.VMEM((heads, 2, half, 128), bf16),
            pltpu.VMEM((heads, 2, 2, half, half), bf16),
            pltpu.VMEM((ncol, count, width), bf16),
            pltpu.VMEM((ncol, count, width), f32),
            pltpu.VMEM((ncol, 2 * width, count), bf16),
            pltpu.VMEM((ncol, count, 2 * width), bf16),
            pltpu.VMEM((ncol, count, 2 * width), f32),
            pltpu.VMEM((ncol, count, width), bf16),
            dma, dma((ncol // GROUP,)), dma, dma, dma, dma((heads, Y - 1)), dma, dma((heads, 2)), dma, dma((heads, 2)),
            dma, dma((heads, 5)), dma, dma,
        ],
        compiler_params=pltpu.CompilerParams(
            collective_id=0, has_side_effects=True, vmem_limit_bytes=56 * 2**20
        ),
        cost_estimate=pl.CostEstimate(flops=4 * 10**9, bytes_accessed=10**7, transcendentals=15 * 10**6),
    )(pair, mask, wqg, wkt, wv, wbt, wo)


def body(pair, token_mask, chain_ids, w_query, w_key, w_value, w_gate, w_bias, w_out):
    rows, cols, width = pair.shape
    heads = w_bias.shape[1]
    count = token_mask.shape[0]
    members = count // rows
    ncol = cols // members
    first = lax.axis_index("col") * cols + lax.axis_index("row") * ncol

    def order(tokens):
        return tokens.reshape(members // 2, 2, rows).swapaxes(0, 1).reshape(count)

    my_chain = lax.dynamic_slice_in_dim(chain_ids, first, ncol)
    keep = (order(token_mask) == 1)[None, :] & (order(chain_ids)[None, :] == my_chain[:, None])
    mask = jnp.where(keep, 0.0, NEG).astype(jnp.float32)
    wbt = jnp.pad(w_bias.T, ((0, 16 - heads), (0, 0)))
    wqg = jnp.concatenate([w_query, w_gate], 1)
    update = exchange(heads, ncol, count, pair, mask, wqg, w_key.T, w_value, wbt, w_out)
    return jnp.swapaxes(update, 0, 1)


def solution(mesh):
    placed = (P("row", "col", None), P(), P(), P(), P(), P(), P(), P(), P())
    return jax.shard_map(
        body, mesh=mesh, in_specs=placed, out_specs=P("row", "col", None), check_vma=False
    )
```

```python
import functools
import math

import jax
import jax.numpy as jnp
from jax import lax
from jax.experimental import pallas as pl
from jax.experimental.pallas import tpu as pltpu
from jax.sharding import PartitionSpec as P

LOG2E = math.log2(math.e)
NT = (((1,), (1,)), ((), ()))
NEG = -1e30
MESH = pl.DeviceIdType.MESH
Z, X = 4, 4
GROUP = 2


def kernel(
    heads,
    pair_ref, token_ref, chains_ref, chain_ref, wq_ref, wk_ref, wv_ref, wg_ref, wb_ref, wo_ref, out_ref,
    normed, bias_f32, sent, x_ref, tiles, bias, q_s, g_s, kt, va, acc, score, back,
    in_send, in_recv, t_send, t_recv, y_send, y_recv, x1_send, x1_recv, x2_send, x2_recv,
    sib_send, sib_recv, out_send, out_recv,
):
    rows, cols, width = pair_ref.shape
    ncol, count, _ = x_ref.shape
    head_dim = width // heads
    members = count // rows
    half = count // 2
    row, col = lax.axis_index("row"), lax.axis_index("col")
    core, z, y_lo = lax.rem(row, 2), lax.rem(row // 2, Z), row // (2 * Z)
    x, y_hi = col // 2, lax.rem(col, 2)
    y = y_hi * 2 + y_lo
    place = row // 2
    slot = core * (members // 2) + place
    sibling = (row + 1 - 2 * core, col)
    right, left = (row, lax.rem(x + 1, X) * 2 + y_hi), (row, lax.rem(x + X - 1, X) * 2 + y_hi)
    x_left, x_right, x_far = lax.rem(x + X - 1, X), lax.rem(x + 1, X), lax.rem(x + 2, X)

    there = lax.rem(y + 3 - 2 * y_lo, 4)
    across = ((lax.rem(there, 2) * Z + z) * 2 + core, x * 2 + there // 2)

    def send(src, dst, send_sem, recv_sem, device):
        pltpu.make_async_remote_copy(
            src_ref=src, dst_ref=dst, send_sem=send_sem, recv_sem=recv_sem, device_id=device, device_id_type=MESH
        ).start()

    def await_bytes(ref, sem):
        pltpu.make_async_copy(ref, ref, sem).wait()

    barrier = pltpu.get_barrier_semaphore()

    def greet(step, _):
        pl.semaphore_signal(barrier, inc=1, device_id=(lax.rem(row + step, members), col), device_id_type=MESH)
        return 0

    lax.fori_loop(1, members, greet, 0)
    for device in (right, left, across):
        pl.semaphore_signal(barrier, inc=1, device_id=device, device_id_type=MESH)

    bias_f32[...] = jnp.zeros_like(bias_f32)
    many = 4

    def norm(t, _):
        values = pair_ref[pl.ds(t * many, many)].reshape(many * cols, width).astype(jnp.float32)
        center = jnp.mean(values, axis=-1, keepdims=True)
        spread = jnp.mean((values - center) ** 2, axis=-1, keepdims=True)
        block = ((values - center) * lax.rsqrt(spread + 1e-05)).astype(jnp.bfloat16)
        normed[pl.ds(pl.multiple_of(t * many * cols, many * cols), many * cols), :] = block.astype(jnp.float32)
        for u in range(many):
            part = block[u * cols : (u + 1) * cols]
            line = lax.dot_general(wb_ref[...], part, NT, preferred_element_type=jnp.float32)
            bias_f32[pl.ds(pl.multiple_of((t * many + u) * 8, 8), heads), :cols] = line
        return 0

    lax.fori_loop(0, rows // many, norm, 0)
    mine = pl.ds(pl.multiple_of(place * rows, rows), rows)
    tiles[mine, :] = jnp.concatenate(
        [bias_f32[pl.ds(h, rows, stride=8), :][:, :cols] for h in range(heads)], axis=1
    ).astype(jnp.bfloat16)

    pl.semaphore_wait(barrier, members + 2)
    for step in range(1, members // 2):
        there = lax.rem(row + 2 * step, members)
        send(tiles.at[mine], tiles.at[mine], t_send, t_recv, (there, col))

    def turn(t, _):
        for u in range(many):
            j = t * many + u
            sent[j] = normed[pl.ds(j, rows, stride=cols), :].astype(jnp.bfloat16)
        return 0

    lax.fori_loop(0, cols // many, turn, 0)
    here = pl.ds(pl.multiple_of(slot * rows, rows), rows)
    for g in range(ncol // GROUP):
        def scatter(step, _, g=g):
            peer = lax.rem(row + step, members)
            send(
                sent.at[pl.ds(peer * ncol + g * GROUP, GROUP)],
                x_ref.at[pl.ds(g * GROUP, GROUP), here],
                in_send, in_recv.at[g], (peer, col),
            )
            return 0

        lax.fori_loop(1, members, scatter, 0)
    for j in range(ncol):
        x_ref[j, here, :] = sent[row * ncol + j]

    await_bytes(tiles.at[pl.ds(0, (members // 2 - 1) * rows)], t_recv)
    wide = cols // 2
    packed = heads * cols
    eye = (
        lax.broadcasted_iota(jnp.int32, (packed, packed), 0) == lax.broadcasted_iota(jnp.int32, (packed, packed), 1)
    ).astype(jnp.bfloat16)
    turned = lax.dot_general(eye, tiles[...], NT, preferred_element_type=jnp.float32).astype(jnp.bfloat16)
    for h in range(heads):
        for part in range(2):
            at = pl.ds(pl.multiple_of(x * cols + y_hi * wide, wide), wide)
            bias[h, core, part, at, :] = turned[h * cols + part * wide : h * cols + (part + 1) * wide]

    def owned(h, owner, side):
        return bias.at[h, core, :, pl.ds(pl.multiple_of(owner * cols + side * wide, wide), wide)]

    near, far = y_hi, 1 - y_hi

    def offer(h, side, n):
        block = owned(h, x, side)
        send(block, block, x1_send, x1_recv.at[h, 0, n], right)
        send(block, block, x1_send, x1_recv.at[h, 1, n], left)
        send(block, block, sib_send, sib_recv.at[h, n], sibling)

    def offer_far(h):
        await_bytes(owned(h, x, far), y_recv.at[h])
        offer(h, far, 1)

    for h in range(heads):
        block = owned(h, x, near)
        send(block, block, y_send, y_recv.at[h], across)
        if h < 2:
            offer(h, near, 0)
    offer_far(0)
    offer(2, near, 0)
    offer_far(1)
    offer(3, near, 0)
    offer_far(2)
    offer_far(3)

    def forward(h):
        for n, (owner, ahead) in enumerate(((x_left, right), (x_right, left))):
            for m, part in enumerate((near, far)):
                block = owned(h, owner, part)
                await_bytes(block, x1_recv.at[h, n, m])
                if n == m:
                    send(block, block, x2_send, x2_recv.at[h, n], ahead)
                send(block, block, sib_send, sib_recv.at[h, 2 + 2 * n + m], sibling)

    def pass_on(h):
        for n, side in enumerate((near, far)):
            block = owned(h, x_far, side)
            await_bytes(block, x2_recv.at[h, n])
            send(block, block, sib_send, sib_recv.at[h, 6 + n], sibling)

    def complete(h):
        for n in range(8):
            await_bytes(owned(h, x, near), sib_recv.at[h, n])

    lane = lax.broadcasted_iota(jnp.int32, (count, width), 1) // head_dim
    one = (lax.broadcasted_iota(jnp.int32, (count, width), 1) == 0).astype(jnp.bfloat16)

    def order(tokens):
        line = tokens.reshape(1, count)
        places = [2 * n + c for c in range(2) for n in range(members // 2)]
        return jnp.concatenate([line[:, n * rows : (n + 1) * rows] for n in places], axis=1)

    real, chains = order(token_ref[...]) == 1, order(chains_ref[...])
    wkt = wk_ref[...].astype(jnp.float32).T.astype(jnp.bfloat16)

    def project(j, _):
        block = x_ref[j]
        q = jnp.dot(block, wq_ref[...], preferred_element_type=jnp.float32)
        q_s[j] = (q * (LOG2E / math.sqrt(head_dim))).astype(jnp.bfloat16)
        g_s[j] = jax.nn.sigmoid(jnp.dot(block, wg_ref[...], preferred_element_type=jnp.float32))
        kt[j, :width, :] = lax.dot_general(wkt, block, NT, preferred_element_type=jnp.float32).astype(
            jnp.bfloat16
        )
        first = lax.broadcasted_iota(jnp.int32, (16, count), 0) == 0
        chain = chain_ref[col * cols + row * ncol + j]
        keep = real & (chains == chain)
        kt[j, width : width + 16, :] = jnp.where(first & ~keep, NEG, 0.0).astype(jnp.bfloat16)
        kt[j, width + 16 :, :] = jnp.zeros((width - 16, count), jnp.bfloat16)
        va[j, :, :width] = jnp.dot(block, wv_ref[...], preferred_element_type=jnp.float32).astype(jnp.bfloat16)
        va[j, :, width:] = jnp.ones((count, width), jnp.bfloat16)
        return 0

    for g in range(ncol // GROUP):
        await_bytes(x_ref.at[pl.ds(0, GROUP), pl.ds(0, count - rows)], in_recv.at[g])
        lax.fori_loop(g * GROUP, (g + 1) * GROUP, project, 0)
        if g == 0:
            forward(0)

    lanes = jnp.concatenate([lane, lane], 1)

    def scores(h, j):
        q = jnp.where(lane == h, q_s[j], jnp.zeros((count, width), jnp.bfloat16))
        s = jnp.dot(jnp.concatenate([q, one], 1), kt[j], preferred_element_type=jnp.float32)
        b = jnp.concatenate([bias[h, n].reshape(count, half) for n in range(2)], 1)
        return s + b.astype(jnp.float32) * LOG2E

    def settle(s, h, j):
        peak = jnp.max(s, axis=1, keepdims=True)
        p = jnp.exp2(s - peak).astype(jnp.bfloat16)
        o = jnp.dot(p, va[j], preferred_element_type=jnp.float32)
        acc[j] = jnp.where(lanes == h, o, acc[j])

    def early(t, _):
        for u in range(2):
            now = 2 * t + u
            later = now + 1
            ahead = scores(later // ncol, lax.rem(later, ncol))
            settle(score[u], now // ncol, lax.rem(now, ncol))
            score[1 - u] = ahead
        return 0

    def late(j, _):
        ahead = scores(heads - 1, j)
        settle(score[0], heads - 2, j)
        score[1] = ahead
        ahead = scores(heads - 2, jnp.minimum(j + 1, ncol - 1))
        settle(score[1], heads - 1, j)
        score[0] = ahead
        o = acc[j]
        gated = (o[:, :width] / o[:, width:] * g_s[j]).astype(jnp.bfloat16)
        back[j] = jnp.dot(gated, wo_ref[...], preferred_element_type=jnp.float32).astype(jnp.bfloat16)

        def give(step, _):
            peer = lax.rem(row + step, members)
            at = (lax.rem(peer, 2) * (members // 2) + peer // 2) * rows
            send(
                back.at[j, pl.ds(pl.multiple_of(at, rows), rows)], out_ref.at[row * ncol + j],
                out_send, out_recv, (peer, col),
            )
            return 0

        lax.fori_loop(1, members, give, 0)
        out_ref[row * ncol + j] = back[j, here, :]
        return 0

    pass_on(0)
    forward(1)
    complete(0)
    score[0] = scores(0, 0)
    lax.fori_loop(0, 2, early, 0)
    pass_on(1)
    forward(2)
    complete(1)
    lax.fori_loop(2, 5, early, 0)
    pass_on(2)
    forward(3)
    complete(2)
    lax.fori_loop(5, 6, early, 0)
    pass_on(3)
    complete(3)
    lax.fori_loop(0, ncol, late, 0)

    await_bytes(out_ref.at[pl.ds(0, (members - 1) * ncol)], out_recv)
    await_bytes(out_ref.at[pl.ds(0, (members - 1) * ncol)], out_send)
    await_bytes(sent.at[pl.ds(0, (members - 1) * ncol)], in_send)
    await_bytes(tiles.at[pl.ds(0, (members // 2 - 1) * rows)], t_send)
    await_bytes(bias.at[0, 0, 0], y_send)
    await_bytes(bias.at[0], x1_send)
    await_bytes(bias.at[0, 0], x2_send)
    await_bytes(bias.at[:, 0], sib_send)


def exchange(heads, ncol, count, pair, token_mask, chain_ids, *weights):
    rows, cols, width = pair.shape
    half = count // 2
    bf16, f32 = jnp.bfloat16, jnp.float32
    dma = pltpu.SemaphoreType.DMA
    return pl.pallas_call(
        functools.partial(kernel, heads),
        out_shape=jax.ShapeDtypeStruct((cols, rows, width), bf16),
        in_specs=[pl.BlockSpec(memory_space=pltpu.SMEM if n == 3 else pltpu.VMEM) for n in range(10)],
        out_specs=pl.BlockSpec(memory_space=pltpu.VMEM),
        scratch_shapes=[
            pltpu.VMEM((rows * cols, width), f32),
            pltpu.VMEM((rows * 8, 128), f32),
            pltpu.VMEM((cols, rows, width), bf16),
            pltpu.VMEM((ncol, count, width), bf16),
            pltpu.VMEM((half, heads * cols), bf16),
            pltpu.VMEM((heads, 2, 2, half, half), bf16),
            pltpu.VMEM((ncol, count, width), bf16),
            pltpu.VMEM((ncol, count, width), f32),
            pltpu.VMEM((ncol, 2 * width, count), bf16),
            pltpu.VMEM((ncol, count, 2 * width), bf16),
            pltpu.VMEM((ncol, count, 2 * width), f32),
            pltpu.VMEM((2, count, count), f32),
            pltpu.VMEM((ncol, count, width), bf16),
            dma, dma((ncol // GROUP,)), dma, dma, dma, dma((heads,)), dma, dma((heads, 2, 2)), dma, dma((heads, 2)),
            dma, dma((heads, 8)), dma, dma,
        ],
        compiler_params=pltpu.CompilerParams(
            collective_id=0, has_side_effects=True, vmem_limit_bytes=56 * 2**20
        ),
        cost_estimate=pl.CostEstimate(flops=4 * 10**9, bytes_accessed=10**7, transcendentals=15 * 10**6),
    )(pair, token_mask, chain_ids, chain_ids, *weights)


def body(pair, token_mask, chain_ids, w_query, w_key, w_value, w_gate, w_bias, w_out):
    rows, cols, width = pair.shape
    heads = w_bias.shape[1]
    count = token_mask.shape[0]
    members = count // rows
    ncol = cols // members
    update = exchange(
        heads, ncol, count, pair, token_mask, chain_ids, w_query, w_key, w_value, w_gate, w_bias.T, w_out
    )
    return jnp.swapaxes(update, 0, 1)


def solution(mesh):
    placed = (P("row", "col", None), P(), P(), P(), P(), P(), P(), P(), P())
    return jax.shard_map(
        body, mesh=mesh, in_specs=placed, out_specs=P("row", "col", None), check_vma=False
    )
```

```python
import functools
import math

import jax
import jax.numpy as jnp
from jax import lax
from jax.experimental import pallas as pl
from jax.experimental.pallas import tpu as pltpu
from jax.sharding import PartitionSpec as P

LOG2E = math.log2(math.e)
NT = (((1,), (1,)), ((), ()))
NEG = -1e30
MESH = pl.DeviceIdType.MESH
Z, X = 4, 4
GROUP = 2


def kernel(
    heads,
    pair_ref, token_ref, chains_ref, chain_ref, wq_ref, wk_ref, wv_ref, wg_ref, wb_ref, wo_ref, out_ref,
    normed, bias_f32, sent, x_ref, tiles, bias, q_s, g_s, kt, va, acc, score, back,
    in_send, in_recv, t_send, t_recv, y_send, y_recv, x1_send, x1_recv, x2_send, x2_recv,
    up_send, down_send, z_recv, sib_send, sib_recv, out_send, out_recv,
):
    rows, cols, width = pair_ref.shape
    ncol, count, _ = x_ref.shape
    head_dim = width // heads
    members = count // rows
    half = count // 2
    row, col = lax.axis_index("row"), lax.axis_index("col")
    core, z, y_lo = lax.rem(row, 2), lax.rem(row // 2, Z), row // (2 * Z)
    x, y_hi = col // 2, lax.rem(col, 2)
    y = y_hi * 2 + y_lo
    place = row // 2
    slot = core * (members // 2) + place
    sibling = (row + 1 - 2 * core, col)
    right, left = (row, lax.rem(x + 1, X) * 2 + y_hi), (row, lax.rem(x + X - 1, X) * 2 + y_hi)
    x_left, x_right, x_far = lax.rem(x + X - 1, X), lax.rem(x + 1, X), lax.rem(x + 2, X)

    there = lax.rem(y + 3 - 2 * y_lo, 4)
    across = ((lax.rem(there, 2) * Z + z) * 2 + core, x * 2 + there // 2)

    up, down = (row - 2 * z + 2 * lax.rem(z + 1, Z), col), (row - 2 * z + 2 * lax.rem(z + Z - 1, Z), col)

    def head_at(n):
        return 2 * lax.rem(z + lax.rem(n, 2), 2) + n // 2

    def send(src, dst, send_sem, recv_sem, device):
        pltpu.make_async_remote_copy(
            src_ref=src, dst_ref=dst, send_sem=send_sem, recv_sem=recv_sem, device_id=device, device_id_type=MESH
        ).start()

    def await_bytes(ref, sem):
        pltpu.make_async_copy(ref, ref, sem).wait()

    barrier = pltpu.get_barrier_semaphore()

    def greet(step, _):
        pl.semaphore_signal(barrier, inc=1, device_id=(lax.rem(row + step, members), col), device_id_type=MESH)
        return 0

    lax.fori_loop(1, members, greet, 0)
    for device in (right, left, across):
        pl.semaphore_signal(barrier, inc=1, device_id=device, device_id_type=MESH)

    bias_f32[...] = jnp.zeros_like(bias_f32)
    many = rows // 4

    def norm(t, _):
        values = pair_ref[pl.ds(t * many, many)].reshape(many * cols, width).astype(jnp.float32)
        center = jnp.mean(values, axis=-1, keepdims=True)
        spread = jnp.mean((values - center) ** 2, axis=-1, keepdims=True)
        block = ((values - center) * lax.rsqrt(spread + 1e-05)).astype(jnp.bfloat16)
        normed[pl.ds(pl.multiple_of(t * many * cols, many * cols), many * cols), :] = block.astype(jnp.float32)
        for u in range(many):
            part = block[u * cols : (u + 1) * cols]
            line = lax.dot_general(wb_ref[...], part, NT, preferred_element_type=jnp.float32)
            bias_f32[pl.ds(pl.multiple_of((t * many + u) * 8, 8), heads), :cols] = line
        return 0

    lax.fori_loop(0, rows // many, norm, 0)
    mine = pl.ds(pl.multiple_of(place * rows, rows), rows)
    tiles[mine, :] = jnp.concatenate(
        [bias_f32[pl.ds(h, rows, stride=8), :][:, :cols] for h in range(heads)], axis=1
    ).astype(jnp.bfloat16)

    pl.semaphore_wait(barrier, members + 2)
    for step in range(1, members // 2):
        there = lax.rem(row + 2 * step, members)
        send(tiles.at[mine], tiles.at[mine], t_send, t_recv, (there, col))

    def turn(t, _):
        for u in range(cols // 8):
            j = t * (cols // 8) + u
            sent[j] = normed[pl.ds(j, rows, stride=cols), :].astype(jnp.bfloat16)
        return 0

    lax.fori_loop(0, 8, turn, 0)
    here = pl.ds(pl.multiple_of(slot * rows, rows), rows)
    for g in range(ncol // GROUP):
        def scatter(step, _, g=g):
            peer = lax.rem(row + step, members)
            send(
                sent.at[pl.ds(peer * ncol + g * GROUP, GROUP)],
                x_ref.at[pl.ds(g * GROUP, GROUP), here],
                in_send, in_recv.at[g], (peer, col),
            )
            return 0

        lax.fori_loop(1, members, scatter, 0)
    for j in range(ncol):
        x_ref[j, here, :] = sent[row * ncol + j]

    await_bytes(tiles.at[pl.ds(0, (members // 2 - 1) * rows)], t_recv)
    wide = cols // 2
    packed = heads * cols
    eye = (
        lax.broadcasted_iota(jnp.int32, (packed, packed), 0) == lax.broadcasted_iota(jnp.int32, (packed, packed), 1)
    ).astype(jnp.bfloat16)
    turned = lax.dot_general(eye, tiles[...], NT, preferred_element_type=jnp.float32).astype(jnp.bfloat16)
    for h in range(heads):
        for part in range(2):
            at = pl.ds(pl.multiple_of(x * cols + y_hi * wide, wide), wide)
            bias[h, core, part, at, :] = turned[h * cols + part * wide : h * cols + (part + 1) * wide]

    def owned(h, owner, side):
        return bias.at[h, core, :, pl.ds(pl.multiple_of(owner * cols + side * wide, wide), wide)]

    near, far = y_hi, 1 - y_hi

    def offer(n, side, m):
        h = head_at(n)
        block = owned(h, x, side)
        if n % 2 == 0:
            send(block, block, x1_send, x1_recv.at[h, 0, m], right)
            send(block, block, x1_send, x1_recv.at[h, 1, m], left)
        send(block, block, sib_send, sib_recv.at[h, m], sibling)

    def offer_far(n):
        h = head_at(n)
        await_bytes(owned(h, x, far), y_recv.at[h])
        offer(n, far, 1)

    for n in (0, 2, 1, 3):
        block = owned(head_at(n), x, near)
        send(block, block, y_send, y_recv.at[head_at(n)], across)
        offer(n, near, 0)
    for n in (0, 2, 1, 3):
        offer_far(n)

    def relay(h, block, n, m):
        send(block, block, sib_send, sib_recv.at[h, 2 + 2 * n + m], sibling)
        if m == 0:
            send(block, block, up_send, z_recv.at[h, n, m], up)
        else:
            send(block, block, down_send, z_recv.at[h, n, m], down)

    def forward(n):
        h = head_at(n)
        for n, (owner, ahead) in enumerate(((x_left, right), (x_right, left))):
            for m, part in enumerate((near, far)):
                block = owned(h, owner, part)
                await_bytes(block, x1_recv.at[h, n, m])
                if n == m:
                    send(block, block, x2_send, x2_recv.at[h, n], ahead)
                relay(h, block, n, m)

    def pass_on(n):
        h = head_at(n)
        for m, part in enumerate((near, far)):
            block = owned(h, x_far, part)
            await_bytes(block, x2_recv.at[h, m])
            relay(h, block, 2, m)

    def accept(n):
        h = head_at(n)
        for n, owner in enumerate((x_left, x_right, x_far)):
            for m, part in enumerate((near, far)):
                block = owned(h, owner, part)
                await_bytes(block, z_recv.at[h, n, m])
                send(block, block, sib_send, sib_recv.at[h, 2 + 2 * n + m], sibling)

    def complete(n):
        h = head_at(n)
        for m in range(8):
            await_bytes(owned(h, x, near), sib_recv.at[h, m])

    lane = lax.broadcasted_iota(jnp.int32, (count, width), 1) // head_dim
    one = (lax.broadcasted_iota(jnp.int32, (count, width), 1) == 0).astype(jnp.bfloat16)

    def order(tokens):
        line = tokens.reshape(1, count)
        places = [2 * n + c for c in range(2) for n in range(members // 2)]
        return jnp.concatenate([line[:, n * rows : (n + 1) * rows] for n in places], axis=1)

    real, chains = order(token_ref[...]) == 1, order(chains_ref[...])
    wkt = wk_ref[...].astype(jnp.float32).T.astype(jnp.bfloat16)

    def project(j, _):
        block = x_ref[j]
        q = jnp.dot(block, wq_ref[...], preferred_element_type=jnp.float32)
        q_s[j] = (q * (LOG2E / math.sqrt(head_dim))).astype(jnp.bfloat16)
        g_s[j] = jax.nn.sigmoid(jnp.dot(block, wg_ref[...], preferred_element_type=jnp.float32))
        kt[j, :width, :] = lax.dot_general(wkt, block, NT, preferred_element_type=jnp.float32).astype(
            jnp.bfloat16
        )
        first = lax.broadcasted_iota(jnp.int32, (16, count), 0) == 0
        chain = chain_ref[col * cols + row * ncol + j]
        keep = real & (chains == chain)
        kt[j, width : width + 16, :] = jnp.where(first & ~keep, NEG, 0.0).astype(jnp.bfloat16)
        kt[j, width + 16 :, :] = jnp.zeros((width - 16, count), jnp.bfloat16)
        va[j, :, :width] = jnp.dot(block, wv_ref[...], preferred_element_type=jnp.float32).astype(jnp.bfloat16)
        va[j, :, width:] = jnp.ones((count, width), jnp.bfloat16)
        return 0

    for g in range(ncol // GROUP):
        await_bytes(x_ref.at[pl.ds(0, GROUP), pl.ds(0, count - rows)], in_recv.at[g])
        lax.fori_loop(g * GROUP, (g + 1) * GROUP, project, 0)
        if g == 0:
            forward(0)
        if g == 1:
            pass_on(0)
            forward(2)

    lanes = jnp.concatenate([lane, lane], 1)

    def scores(h, j):
        q = jnp.where(lane == h, q_s[j], jnp.zeros((count, width), jnp.bfloat16))
        s = jnp.dot(jnp.concatenate([q, one], 1), kt[j], preferred_element_type=jnp.float32)
        b = jnp.concatenate([bias[h, n].reshape(count, half) for n in range(2)], 1)
        return s + b.astype(jnp.float32) * LOG2E

    def settle(s, h, j):
        peak = jnp.max(s, axis=1, keepdims=True)
        p = jnp.exp2(s - peak).astype(jnp.bfloat16)
        o = jnp.dot(p, va[j], preferred_element_type=jnp.float32)
        acc[j] = jnp.where(lanes == h, o, acc[j])

    def early(t, _):
        for u in range(2):
            now = 2 * t + u
            later = now + 1
            ahead = scores(head_at(later // ncol), lax.rem(later, ncol))
            settle(score[u], head_at(now // ncol), lax.rem(now, ncol))
            score[1 - u] = ahead
        return 0

    def late(j, _):
        ahead = scores(head_at(heads - 1), j)
        settle(score[0], head_at(heads - 2), j)
        score[1] = ahead
        ahead = scores(head_at(heads - 2), jnp.minimum(j + 1, ncol - 1))
        settle(score[1], head_at(heads - 1), j)
        score[0] = ahead
        o = acc[j]
        gated = (o[:, :width] / o[:, width:] * g_s[j]).astype(jnp.bfloat16)
        back[j] = jnp.dot(gated, wo_ref[...], preferred_element_type=jnp.float32).astype(jnp.bfloat16)

        def give(step, _):
            peer = lax.rem(row + step, members)
            at = (lax.rem(peer, 2) * (members // 2) + peer // 2) * rows
            send(
                back.at[j, pl.ds(pl.multiple_of(at, rows), rows)], out_ref.at[row * ncol + j],
                out_send, out_recv, (peer, col),
            )
            return 0

        lax.fori_loop(1, members, give, 0)
        out_ref[row * ncol + j] = back[j, here, :]
        return 0

    complete(0)
    score[0] = scores(head_at(0), 0)
    lax.fori_loop(0, 1, early, 0)
    accept(1)
    pass_on(2)
    lax.fori_loop(1, 2, early, 0)
    complete(1)
    lax.fori_loop(2, 4, early, 0)
    accept(3)
    lax.fori_loop(4, 5, early, 0)
    complete(2)
    lax.fori_loop(5, 6, early, 0)
    complete(3)
    lax.fori_loop(0, ncol, late, 0)

    await_bytes(out_ref.at[pl.ds(0, (members - 1) * ncol)], out_recv)
    await_bytes(out_ref.at[pl.ds(0, (members - 1) * ncol)], out_send)
    await_bytes(sent.at[pl.ds(0, (members - 1) * ncol)], in_send)
    await_bytes(tiles.at[pl.ds(0, (members // 2 - 1) * rows)], t_send)
    await_bytes(bias.at[0, 0, 0], y_send)
    await_bytes(bias.at[0, 0], x1_send)
    await_bytes(bias.at[0, 0, 0], x2_send)
    await_bytes(bias.at[0, 0, :, pl.ds(0, 3 * cols)], up_send)
    await_bytes(bias.at[0, 0, :, pl.ds(0, 3 * cols)], down_send)
    await_bytes(bias.at[:, 0], sib_send)


def exchange(heads, ncol, count, pair, token_mask, chain_ids, *weights):
    rows, cols, width = pair.shape
    half = count // 2
    bf16, f32 = jnp.bfloat16, jnp.float32
    dma = pltpu.SemaphoreType.DMA
    return pl.pallas_call(
        functools.partial(kernel, heads),
        out_shape=jax.ShapeDtypeStruct((cols, rows, width), bf16),
        in_specs=[pl.BlockSpec(memory_space=pltpu.SMEM if n == 3 else pltpu.VMEM) for n in range(10)],
        out_specs=pl.BlockSpec(memory_space=pltpu.VMEM),
        scratch_shapes=[
            pltpu.VMEM((rows * cols, width), f32),
            pltpu.VMEM((rows * 8, 128), f32),
            pltpu.VMEM((cols, rows, width), bf16),
            pltpu.VMEM((ncol, count, width), bf16),
            pltpu.VMEM((half, heads * cols), bf16),
            pltpu.VMEM((heads, 2, 2, half, half), bf16),
            pltpu.VMEM((ncol, count, width), bf16),
            pltpu.VMEM((ncol, count, width), f32),
            pltpu.VMEM((ncol, 2 * width, count), bf16),
            pltpu.VMEM((ncol, count, 2 * width), bf16),
            pltpu.VMEM((ncol, count, 2 * width), f32),
            pltpu.VMEM((2, count, count), f32),
            pltpu.VMEM((ncol, count, width), bf16),
            dma, dma((ncol // GROUP,)), dma, dma, dma, dma((heads,)), dma, dma((heads, 2, 2)), dma, dma((heads, 2)),
            dma, dma, dma((heads, 3, 2)), dma, dma((heads, 8)), dma, dma,
        ],
        compiler_params=pltpu.CompilerParams(
            collective_id=0, has_side_effects=True, vmem_limit_bytes=56 * 2**20
        ),
        cost_estimate=pl.CostEstimate(flops=4 * 10**9, bytes_accessed=10**7, transcendentals=15 * 10**6),
    )(pair, token_mask, chain_ids, chain_ids, *weights)


def body(pair, token_mask, chain_ids, w_query, w_key, w_value, w_gate, w_bias, w_out):
    rows, cols, width = pair.shape
    heads = w_bias.shape[1]
    count = token_mask.shape[0]
    members = count // rows
    ncol = cols // members
    update = exchange(
        heads, ncol, count, pair, token_mask, chain_ids, w_query, w_key, w_value, w_gate, w_bias.T, w_out
    )
    return jnp.swapaxes(update, 0, 1)


def solution(mesh):
    placed = (P("row", "col", None), P(), P(), P(), P(), P(), P(), P(), P())
    return jax.shard_map(
        body, mesh=mesh, in_specs=placed, out_specs=P("row", "col", None), check_vma=False
    )
```

```python
import functools
import math

import jax
import jax.numpy as jnp
from jax import lax
from jax.experimental import pallas as pl
from jax.experimental.pallas import tpu as pltpu
from jax.sharding import PartitionSpec as P

LOG2E = math.log2(math.e)
NT = (((1,), (1,)), ((), ()))
NEG = -1e30
MESH = pl.DeviceIdType.MESH
Z, X = 4, 4
GROUP = 2


def kernel(
    heads,
    pair_ref, token_ref, chains_ref, chain_ref, wq_ref, wk_ref, wv_ref, wg_ref, wb_ref, wo_ref, out_ref,
    normed, bias_f32, sent, x_ref, tiles, bias, q_s, g_s, kt, va, acc, score, back,
    in_send, in_recv, t_send, t_recv, y_send, y_recv, x1_send, x1_recv, x2_send, x2_recv,
    up_send, down_send, z_recv, sib_send, sib_recv, out_send, out_recv,
):
    rows, cols, width = pair_ref.shape
    ncol, count, _ = x_ref.shape
    head_dim = width // heads
    members = count // rows
    half = count // 2
    row, col = lax.axis_index("row"), lax.axis_index("col")
    core, z, y_lo = lax.rem(row, 2), lax.rem(row // 2, Z), row // (2 * Z)
    x, y_hi = col // 2, lax.rem(col, 2)
    y = y_hi * 2 + y_lo
    place = row // 2
    slot = core * (members // 2) + place
    sibling = (row + 1 - 2 * core, col)
    right, left = (row, lax.rem(x + 1, X) * 2 + y_hi), (row, lax.rem(x + X - 1, X) * 2 + y_hi)
    x_left, x_right, x_far = lax.rem(x + X - 1, X), lax.rem(x + 1, X), lax.rem(x + 2, X)

    there = lax.rem(y + 3 - 2 * y_lo, 4)
    across = ((lax.rem(there, 2) * Z + z) * 2 + core, x * 2 + there // 2)

    up, down = (row - 2 * z + 2 * lax.rem(z + 1, Z), col), (row - 2 * z + 2 * lax.rem(z + Z - 1, Z), col)

    def head_at(n):
        return 2 * lax.rem(z + lax.rem(n, 2), 2) + n // 2

    def send(src, dst, send_sem, recv_sem, device):
        pltpu.make_async_remote_copy(
            src_ref=src, dst_ref=dst, send_sem=send_sem, recv_sem=recv_sem, device_id=device, device_id_type=MESH
        ).start()

    def await_bytes(ref, sem):
        pltpu.make_async_copy(ref, ref, sem).wait()

    barrier = pltpu.get_barrier_semaphore()

    def greet(step, _):
        pl.semaphore_signal(barrier, inc=1, device_id=(lax.rem(row + step, members), col), device_id_type=MESH)
        return 0

    lax.fori_loop(1, members, greet, 0)
    for device in (right, left, across):
        pl.semaphore_signal(barrier, inc=1, device_id=device, device_id_type=MESH)

    bias_f32[...] = jnp.zeros_like(bias_f32)
    many = rows // 3

    def norm(t, _):
        values = pair_ref[pl.ds(t * many, many)].reshape(many * cols, width).astype(jnp.float32)
        center = jnp.mean(values, axis=-1, keepdims=True)
        spread = jnp.mean((values - center) ** 2, axis=-1, keepdims=True)
        block = ((values - center) * lax.rsqrt(spread + 1e-05)).astype(jnp.bfloat16)
        normed[pl.ds(pl.multiple_of(t * many * cols, many * cols), many * cols), :] = block.astype(jnp.float32)
        for u in range(many):
            part = block[u * cols : (u + 1) * cols]
            line = lax.dot_general(wb_ref[...], part, NT, preferred_element_type=jnp.float32)
            bias_f32[pl.ds(pl.multiple_of((t * many + u) * 8, 8), heads), :cols] = line
        return 0

    lax.fori_loop(0, rows // many, norm, 0)
    mine = pl.ds(pl.multiple_of(place * rows, rows), rows)
    tiles[mine, :] = jnp.concatenate(
        [bias_f32[pl.ds(h, rows, stride=8), :][:, :cols] for h in range(heads)], axis=1
    ).astype(jnp.bfloat16)

    pl.semaphore_wait(barrier, members + 2)
    for step in range(1, members // 2):
        there = lax.rem(row + 2 * step, members)
        send(tiles.at[mine], tiles.at[mine], t_send, t_recv, (there, col))

    def turn(t, _):
        for u in range(cols // 8):
            j = t * (cols // 8) + u
            sent[j] = normed[pl.ds(j, rows, stride=cols), :].astype(jnp.bfloat16)
        return 0

    lax.fori_loop(0, 8, turn, 0)
    here = pl.ds(pl.multiple_of(slot * rows, rows), rows)
    for g in range(ncol // GROUP):
        def scatter(step, _, g=g):
            peer = lax.rem(row + step, members)
            send(
                sent.at[pl.ds(peer * ncol + g * GROUP, GROUP)],
                x_ref.at[pl.ds(g * GROUP, GROUP), here],
                in_send, in_recv.at[g], (peer, col),
            )
            return 0

        lax.fori_loop(1, members, scatter, 0)
    for j in range(ncol):
        x_ref[j, here, :] = sent[row * ncol + j]

    await_bytes(tiles.at[pl.ds(0, (members // 2 - 1) * rows)], t_recv)
    wide = cols // 2
    packed = heads * cols
    eye = (
        lax.broadcasted_iota(jnp.int32, (packed, packed), 0) == lax.broadcasted_iota(jnp.int32, (packed, packed), 1)
    ).astype(jnp.bfloat16)
    turned = lax.dot_general(eye, tiles[...], NT, preferred_element_type=jnp.float32).astype(jnp.bfloat16)
    for h in range(heads):
        for part in range(2):
            at = pl.ds(pl.multiple_of(x * cols + y_hi * wide, wide), wide)
            bias[h, core, part, at, :] = turned[h * cols + part * wide : h * cols + (part + 1) * wide]

    def owned(h, owner, side):
        return bias.at[h, core, :, pl.ds(pl.multiple_of(owner * cols + side * wide, wide), wide)]

    near, far = y_hi, 1 - y_hi

    def offer(n, side, m):
        h = head_at(n)
        block = owned(h, x, side)
        if n % 2 == 0:
            send(block, block, x1_send, x1_recv.at[h, 0, m], right)
            send(block, block, x1_send, x1_recv.at[h, 1, m], left)
        send(block, block, sib_send, sib_recv.at[h, m], sibling)

    def offer_far(n):
        h = head_at(n)
        await_bytes(owned(h, x, far), y_recv.at[h])
        offer(n, far, 1)

    for n in (0, 2, 1, 3):
        block = owned(head_at(n), x, near)
        send(block, block, y_send, y_recv.at[head_at(n)], across)
        offer(n, near, 0)
    for n in (0, 2, 1, 3):
        offer_far(n)

    def relay(h, block, n, m):
        send(block, block, sib_send, sib_recv.at[h, 2 + 2 * n + m], sibling)
        if m == 0:
            send(block, block, up_send, z_recv.at[h, n, m], up)
        else:
            send(block, block, down_send, z_recv.at[h, n, m], down)

    def forward(n):
        h = head_at(n)
        for n, (owner, ahead) in enumerate(((x_left, right), (x_right, left))):
            for m, part in enumerate((near, far)):
                block = owned(h, owner, part)
                await_bytes(block, x1_recv.at[h, n, m])
                if n == m:
                    send(block, block, x2_send, x2_recv.at[h, n], ahead)
                relay(h, block, n, m)

    def pass_on(n):
        h = head_at(n)
        for m, part in enumerate((near, far)):
            block = owned(h, x_far, part)
            await_bytes(block, x2_recv.at[h, m])
            relay(h, block, 2, m)

    def accept(n):
        h = head_at(n)
        for n, owner in enumerate((x_left, x_right, x_far)):
            for m, part in enumerate((near, far)):
                block = owned(h, owner, part)
                await_bytes(block, z_recv.at[h, n, m])
                send(block, block, sib_send, sib_recv.at[h, 2 + 2 * n + m], sibling)

    def complete(n):
        h = head_at(n)
        for m in range(8):
            await_bytes(owned(h, x, near), sib_recv.at[h, m])

    lane = lax.broadcasted_iota(jnp.int32, (count, width), 1) // head_dim
    one = (lax.broadcasted_iota(jnp.int32, (count, width), 1) == 0).astype(jnp.bfloat16)

    def order(tokens):
        line = tokens.reshape(1, count)
        places = [2 * n + c for c in range(2) for n in range(members // 2)]
        return jnp.concatenate([line[:, n * rows : (n + 1) * rows] for n in places], axis=1)

    real, chains = order(token_ref[...]) == 1, order(chains_ref[...])
    wkt = wk_ref[...].astype(jnp.float32).T.astype(jnp.bfloat16)

    def project(j, _):
        block = x_ref[j]
        q = jnp.dot(block, wq_ref[...], preferred_element_type=jnp.float32)
        q_s[j] = (q * (LOG2E / math.sqrt(head_dim))).astype(jnp.bfloat16)
        g_s[j] = jax.nn.sigmoid(jnp.dot(block, wg_ref[...], preferred_element_type=jnp.float32))
        kt[j, :width, :] = lax.dot_general(wkt, block, NT, preferred_element_type=jnp.float32).astype(
            jnp.bfloat16
        )
        first = lax.broadcasted_iota(jnp.int32, (16, count), 0) == 0
        chain = chain_ref[col * cols + row * ncol + j]
        keep = real & (chains == chain)
        kt[j, width : width + 16, :] = jnp.where(first & ~keep, NEG, 0.0).astype(jnp.bfloat16)
        kt[j, width + 16 :, :] = jnp.zeros((width - 16, count), jnp.bfloat16)
        va[j, :, :width] = jnp.dot(block, wv_ref[...], preferred_element_type=jnp.float32).astype(jnp.bfloat16)
        va[j, :, width:] = jnp.ones((count, width), jnp.bfloat16)
        return 0

    for g in range(ncol // GROUP):
        await_bytes(x_ref.at[pl.ds(0, GROUP), pl.ds(0, count - rows)], in_recv.at[g])
        lax.fori_loop(g * GROUP, (g + 1) * GROUP, project, 0)
        if g == 0:
            forward(0)
        if g == 1:
            pass_on(0)
            forward(2)

    lanes = jnp.concatenate([lane, lane], 1)

    def scores(h, j):
        q = jnp.where(lane == h, q_s[j], jnp.zeros((count, width), jnp.bfloat16))
        s = jnp.dot(jnp.concatenate([q, one], 1), kt[j], preferred_element_type=jnp.float32)
        b = jnp.concatenate([bias[h, n].reshape(count, half) for n in range(2)], 1)
        return s + b.astype(jnp.float32) * LOG2E

    def settle(s, h, j):
        peak = jnp.max(s, axis=1, keepdims=True)
        p = jnp.exp2(s - peak).astype(jnp.bfloat16)
        o = jnp.dot(p, va[j], preferred_element_type=jnp.float32)
        acc[j] = jnp.where(lanes == h, o, acc[j])

    def early(t, _):
        for u in range(2):
            now = 2 * t + u
            later = now + 1
            ahead = scores(head_at(later // ncol), lax.rem(later, ncol))
            settle(score[u], head_at(now // ncol), lax.rem(now, ncol))
            score[1 - u] = ahead
        return 0

    def late(j, _):
        ahead = scores(head_at(heads - 1), j)
        settle(score[0], head_at(heads - 2), j)
        score[1] = ahead
        ahead = scores(head_at(heads - 2), jnp.minimum(j + 1, ncol - 1))
        settle(score[1], head_at(heads - 1), j)
        score[0] = ahead
        o = acc[j]
        gated = (o[:, :width] / o[:, width:] * g_s[j]).astype(jnp.bfloat16)
        back[j] = jnp.dot(gated, wo_ref[...], preferred_element_type=jnp.float32).astype(jnp.bfloat16)

        def give(step, _):
            peer = lax.rem(row + step, members)
            at = (lax.rem(peer, 2) * (members // 2) + peer // 2) * rows
            send(
                back.at[j, pl.ds(pl.multiple_of(at, rows), rows)], out_ref.at[row * ncol + j],
                out_send, out_recv, (peer, col),
            )
            return 0

        lax.fori_loop(1, members, give, 0)
        out_ref[row * ncol + j] = back[j, here, :]
        return 0

    complete(0)
    score[0] = scores(head_at(0), 0)
    lax.fori_loop(0, 1, early, 0)
    accept(1)
    pass_on(2)
    lax.fori_loop(1, 2, early, 0)
    complete(1)
    lax.fori_loop(2, 4, early, 0)
    accept(3)
    lax.fori_loop(4, 5, early, 0)
    complete(2)
    lax.fori_loop(5, 6, early, 0)
    complete(3)
    lax.fori_loop(0, ncol, late, 0)

    await_bytes(out_ref.at[pl.ds(0, (members - 1) * ncol)], out_recv)
    await_bytes(out_ref.at[pl.ds(0, (members - 1) * ncol)], out_send)
    await_bytes(sent.at[pl.ds(0, (members - 1) * ncol)], in_send)
    await_bytes(tiles.at[pl.ds(0, (members // 2 - 1) * rows)], t_send)
    await_bytes(bias.at[0, 0, 0], y_send)
    await_bytes(bias.at[0, 0], x1_send)
    await_bytes(bias.at[0, 0, 0], x2_send)
    await_bytes(bias.at[0, 0, :, pl.ds(0, 3 * cols)], up_send)
    await_bytes(bias.at[0, 0, :, pl.ds(0, 3 * cols)], down_send)
    await_bytes(bias.at[:, 0], sib_send)


def exchange(heads, ncol, count, pair, token_mask, chain_ids, *weights):
    rows, cols, width = pair.shape
    half = count // 2
    bf16, f32 = jnp.bfloat16, jnp.float32
    dma = pltpu.SemaphoreType.DMA
    return pl.pallas_call(
        functools.partial(kernel, heads),
        out_shape=jax.ShapeDtypeStruct((cols, rows, width), bf16),
        in_specs=[pl.BlockSpec(memory_space=pltpu.SMEM if n == 3 else pltpu.VMEM) for n in range(10)],
        out_specs=pl.BlockSpec(memory_space=pltpu.VMEM),
        scratch_shapes=[
            pltpu.VMEM((rows * cols, width), f32),
            pltpu.VMEM((rows * 8, 128), f32),
            pltpu.VMEM((cols, rows, width), bf16),
            pltpu.VMEM((ncol, count, width), bf16),
            pltpu.VMEM((half, heads * cols), bf16),
            pltpu.VMEM((heads, 2, 2, half, half), bf16),
            pltpu.VMEM((ncol, count, width), bf16),
            pltpu.VMEM((ncol, count, width), f32),
            pltpu.VMEM((ncol, 2 * width, count), bf16),
            pltpu.VMEM((ncol, count, 2 * width), bf16),
            pltpu.VMEM((ncol, count, 2 * width), f32),
            pltpu.VMEM((2, count, count), f32),
            pltpu.VMEM((ncol, count, width), bf16),
            dma, dma((ncol // GROUP,)), dma, dma, dma, dma((heads,)), dma, dma((heads, 2, 2)), dma, dma((heads, 2)),
            dma, dma, dma((heads, 3, 2)), dma, dma((heads, 8)), dma, dma,
        ],
        compiler_params=pltpu.CompilerParams(
            collective_id=0, has_side_effects=True, vmem_limit_bytes=56 * 2**20
        ),
        cost_estimate=pl.CostEstimate(flops=4 * 10**9, bytes_accessed=10**7, transcendentals=15 * 10**6),
    )(pair, token_mask, chain_ids, chain_ids, *weights)


def body(pair, token_mask, chain_ids, w_query, w_key, w_value, w_gate, w_bias, w_out):
    rows, cols, width = pair.shape
    heads = w_bias.shape[1]
    count = token_mask.shape[0]
    members = count // rows
    ncol = cols // members
    update = exchange(
        heads, ncol, count, pair, token_mask, chain_ids, w_query, w_key, w_value, w_gate, w_bias.T, w_out
    )
    return jnp.swapaxes(update, 0, 1)


def solution(mesh):
    placed = (P("row", "col", None), P(), P(), P(), P(), P(), P(), P(), P())
    return jax.shard_map(
        body, mesh=mesh, in_specs=placed, out_specs=P("row", "col", None), check_vma=False
    )
```
